32 devices in a mesh: node: 16 (over z, x, core), group: 2 (over y).
Axes of the slice: x: 2, y: 2, z: 4, core: 2. Of those that a mesh axis runs over, the one named last changes fastest.
Arguments:
- node_feats: bfloat16 [65536, 256], P(('node', 'group')), may hold values from -24 to 24
- w_query: bfloat16 [256, 256], replicated, may hold values from -0.375 to 0.375
- w_key: bfloat16 [256, 256], replicated, may hold values from -0.375 to 0.375
- w_value: bfloat16 [256, 256], replicated, may hold values from -0.375 to 0.375
- w_graph: bfloat16 [256, 256], replicated, may hold values from -0.375 to 0.375
- src_index: int32 [16, 2, 16, 256], P('node', 'group'), may hold values from 0 to 2047
- dst_slot: int32 [16, 2, 16, 256], P('node', 'group'), may hold values from 0 to 2047
- edge_weight: bfloat16 [16, 2, 16, 256], P('node', 'group'), may hold values from 0.049804688 to 0.5
- tile_count: int32 [16, 2, 16], P('node', 'group'), may hold values from 0 to 2, as said below
Outputs:
- layer_out: bfloat16 [65536, 256], P(('node', 'group'))
The draws below stay inside these ranges and needn't reach their ends.
Inputs may be any that keep to these rules, and one draw needn't show every extreme that they name: `tile_count`: in every group some owner receives 2 tiles from every source device.
All inputs are finite; a program needn't handle non-finite values.
Results may differ from the reference program's by a relative error of at most 0.0047.
Values may be sent and summed in bfloat16 or wider, within the bound.
A program may use at most 64 MiB of HBM per device.

```python
import math
import jax
import jax.numpy as jnp
from jax import lax

D = 256
NODE_DEV = 2048
CAP = 2
TILE = 128
NODES = 65536
N_NODE = 16
N_GROUP = 2


def draw_node_feats(key, part):
    key_a, key_b, key_c = jax.random.split(key, 3)
    devices = NODES // NODE_DEV
    device_of = jnp.arange(NODES) // NODE_DEV
    level = 3.0 ** (device_of.astype(jnp.float32) / max(devices - 1, 1))
    offsets = 0.6 * jnp.clip(jax.random.normal(key_a, (devices, D), jnp.float32), -4.0, 4.0)
    offsets = jnp.repeat(offsets, NODE_DEV, axis=0)
    rowscale = jnp.exp(jax.random.uniform(key_b, (NODES, 1), jnp.float32, -0.7, 0.7))
    noise = jnp.clip(jax.random.normal(key_c, (NODES, D), jnp.float32), -4.0, 4.0)
    values = level[:, None] * rowscale * (noise + offsets)
    return jnp.clip(values, -24.0, 24.0).astype(jnp.bfloat16)


def draw_tile_count(key, part):
    key_a, key_b = jax.random.split(key, 2)
    base = jax.random.randint(key_a, (N_NODE, N_GROUP, N_NODE), 0, CAP + 1)
    heavy = jax.random.randint(key_b, (N_GROUP,), 0, N_NODE)
    owner = jnp.arange(N_NODE)
    full = owner[None, None, :] == heavy[None, :, None]
    return jnp.where(full, CAP, base).astype(jnp.int32)


def touch_ends(entries, key, smallest, top_value):
    longest = entries.shape.index(max(entries.shape))
    spots = []
    for shift in (0, 1):
        where = [jax.random.randint(jax.random.fold_in(key, axis), (), 0, length) for axis, length in enumerate(entries.shape)]
        where[longest] = (where[longest] + shift) % entries.shape[longest]
        spots.append(tuple(where))
    return entries.at[spots[0]].set(smallest).at[spots[1]].set(top_value)


def block_scale(key, extent, shards, least, largest):
    def one(axis_at, shards_of):
        heights = jax.random.uniform(jax.random.fold_in(jax.random.fold_in(key, 6), axis_at), (shards_of,), jnp.float32, least / len(shards), largest / len(shards))
        return jnp.repeat(jnp.exp(heights), extent[axis_at] // shards_of).reshape((-1,) + (1,) * (len(extent) - axis_at - 1))

    loudness = one(*shards[0])
    for cut in shards[1:]:
        loudness = loudness * one(*cut)
    return loudness


def normal_values(own_key, shape, deviation, most, held_as=jnp.bfloat16):
    drawn = deviation * jax.random.normal(own_key, shape, jnp.float32)
    return jnp.clip(drawn, min=-most, max=most).astype(held_as)


def setup_inputs(seed: int = 0) -> dict:
    key_list = jax.random.split(jax.random.key(seed), 10)
    node_feats = draw_node_feats(jax.random.fold_in(key_list[9], 71), 0)
    w_query = normal_values(key_list[1], (D, D), D ** -0.5, 0.375)
    w_key = normal_values(key_list[2], (D, D), D ** -0.5, 0.375)
    w_value = normal_values(key_list[3], (D, D), D ** -0.5, 0.375)
    w_graph = normal_values(key_list[4], (D, D), D ** -0.5, 0.375)
    src_index = touch_ends(jax.random.randint(key_list[5], (N_NODE, N_GROUP, N_NODE, CAP * TILE), 0, NODE_DEV), jax.random.fold_in(key_list[5], 1), 0, NODE_DEV - 1).astype(jnp.int32)
    dst_slot = touch_ends(jax.random.randint(key_list[6], (N_NODE, N_GROUP, N_NODE, CAP * TILE), 0, NODE_DEV), jax.random.fold_in(key_list[6], 1), 0, NODE_DEV - 1).astype(jnp.int32)
    edge_weight = jnp.clip(jnp.exp(math.log(0.5) - 2.306499 * jax.random.uniform(key_list[7], (N_NODE, N_GROUP, N_NODE, CAP * TILE), jnp.float32) ** block_scale(key_list[7], (N_NODE, N_GROUP, N_NODE, CAP * TILE), ((0, 16), (1, 2)), -0.2, 0.2)), 0.049804688, 0.5).astype(jnp.bfloat16)
    tile_count = draw_tile_count(jax.random.fold_in(key_list[9], 71), 0)
    return dict(node_feats=node_feats, w_query=w_query, w_key=w_key, w_value=w_value, w_graph=w_graph, src_index=src_index, dst_slot=dst_slot, edge_weight=edge_weight, tile_count=tile_count)


def reference(node_feats, w_query, w_key, w_value, w_graph, src_index, dst_slot, edge_weight, tile_count):
    slot_rows = CAP * TILE
    sources = N_NODE * N_GROUP
    feats = node_feats.reshape(sources, NODE_DEV, D)
    src_flat = src_index.reshape(sources, N_NODE, slot_rows)
    slot_flat = dst_slot.reshape(sources, N_NODE, slot_rows)
    weight_flat = edge_weight.reshape(sources, N_NODE, slot_rows)
    count_flat = tile_count.reshape(sources, N_NODE)
    group_of = (jnp.arange(sources, dtype=jnp.int32) % N_GROUP).astype(jnp.int32)
    tile_of = (jnp.arange(slot_rows, dtype=jnp.int32) // TILE).astype(jnp.int32)
    owner_base = (jnp.arange(N_NODE, dtype=jnp.int32) * NODE_DEV).astype(jnp.int32)

    def one_source(total, items):
        rows, src, slot, weight, count, group = items
        live = tile_of[None, :] < count[:, None]
        target = jnp.where(live, owner_base[:, None] + slot, N_NODE * NODE_DEV).astype(jnp.int32)
        picked = jnp.take(rows, src.reshape(-1), axis=0).astype(jnp.float32)
        values = picked * weight.reshape(-1, 1).astype(jnp.float32)
        total = total.at[group, target.reshape(-1)].add(values, mode="drop")
        return total, None

    start = jnp.zeros((N_GROUP, N_NODE * NODE_DEV, D), jnp.float32)
    agg, _ = lax.scan(one_source, start, (feats, src_flat, slot_flat, weight_flat, count_flat, group_of))
    agg = agg.reshape(N_GROUP, N_NODE, NODE_DEV, D).transpose(1, 0, 2, 3).reshape(NODES, D)
    agg_b = agg.astype(jnp.bfloat16)
    gcn = jnp.dot(agg_b, w_graph, preferred_element_type=jnp.float32)
    phi_q = jax.nn.elu(jnp.dot(node_feats, w_query, preferred_element_type=jnp.float32)) + 1.0
    phi_k = jax.nn.elu(jnp.dot(node_feats, w_key, preferred_element_type=jnp.float32)) + 1.0
    key_b = phi_k.astype(jnp.bfloat16)
    value_b = jnp.dot(node_feats, w_value, preferred_element_type=jnp.float32).astype(jnp.bfloat16)
    kv = jnp.dot(key_b.T, value_b, preferred_element_type=jnp.float32)
    ksum = jnp.sum(phi_k, axis=0)
    numer = jnp.dot(phi_q, kv, precision=lax.Precision.HIGHEST)
    denom = jnp.dot(phi_q, ksum, precision=lax.Precision.HIGHEST)
    attn = numer / denom[:, None]
    return (0.5 * attn + 0.5 * gcn).astype(jnp.bfloat16)
```

```python
import functools

import jax
import jax.numpy as jnp
from jax import lax
from jax.experimental import pallas as pl
from jax.experimental.pallas import tpu as pltpu
from jax.sharding import PartitionSpec as P

TILE = 128
BLK = 256
META = 16
F32 = jnp.float32
BF16 = jnp.bfloat16
MESH = pl.DeviceIdType.MESH


def kernel(
    nodes, groups, reducers, batch,
    feats, w_query, w_key, w_value, w_graph, src_index, dst_slot, edge_weight, tile_count,
    out,
    outgoing, incoming, src_hi, src_lo, acc, q_hi, q_lo, kv_local, kv_parts, kv_total,
    edge_send, edge_recv, part_send, part_recv, total_send, total_recv,
):
    total = nodes * groups
    step = total // reducers
    rows, width = feats.shape
    slots = src_index.shape[3]
    blocks = rows // BLK
    chunk = width // reducers
    node = lax.axis_index("node")
    group = lax.axis_index("group")
    me = node * groups + group
    mine = me // step
    is_reducer = lax.rem(me, step) == 0

    barrier = pltpu.get_barrier_semaphore()

    def greet(j, _):
        peer = lax.rem(me + j, total)
        pl.semaphore_signal(
            barrier, inc=1, device_id=(peer // groups, lax.rem(peer, groups)), device_id_type=MESH
        )
        return 0

    lax.fori_loop(1, total, greet, 0)

    sources = src_index[0, 0]
    spread = (
        lax.broadcasted_iota(jnp.int32, (nodes, nodes * 128), 0)
        == lax.broadcasted_iota(jnp.int32, (nodes, nodes * 128), 1) // 128
    ).astype(F32).astype(BF16)
    for value, ref in ((sources // BLK, src_hi), (lax.rem(sources, BLK), src_lo)):
        columns = jnp.transpose(value.astype(F32)).astype(BF16)
        ref[...] = jnp.dot(columns, spread, preferred_element_type=F32).astype(BF16)

    lanes = lax.broadcasted_iota(jnp.int32, (slots, 128), 1).astype(F32)
    lane_of = (lanes.astype(BF16), (lanes + 128.0).astype(BF16))
    one, zero = jnp.ones((), BF16), jnp.zeros((), BF16)
    tile_of = lax.broadcasted_iota(jnp.int32, (1, slots), 1) // TILE
    meta_row = lax.broadcasted_iota(jnp.int32, (META, slots), 0)

    def pick(owner, put):
        start = pl.multiple_of(owner * 128, 128)
        high = src_hi[:, pl.ds(start, 128)]
        low = src_lo[:, pl.ds(start, 128)]
        picked = jnp.zeros((slots, width), F32)
        for b in range(blocks):
            local = jnp.where(high == jnp.array(b, BF16), low, jnp.array(-1.0, BF16))
            table = jnp.concatenate(
                [jnp.where(local == lane, one, zero) for lane in lane_of], axis=1
            )
            picked += jnp.dot(table, feats[b * BLK:(b + 1) * BLK, :], preferred_element_type=F32)
        put[0:slots, :] = picked.astype(BF16)
        slot = dst_slot[0, 0, pl.ds(owner, 1), :]
        weight = edge_weight[0, 0, pl.ds(owner, 1), :]
        weight = jnp.where(tile_of < tile_count[owner], weight, 0.0)
        meta = jnp.where(meta_row == 0, weight, 0.0)
        meta = jnp.where(meta_row == 1, (slot // BLK).astype(F32), meta)
        meta = jnp.where(meta_row == 2, lax.rem(slot, BLK).astype(F32), meta)
        put[slots:slots + META, :] = meta.astype(BF16)

    pick(node, incoming.at[0])
    pl.semaphore_wait(barrier, total - 1)

    def edge_copy(k):
        return pltpu.make_async_remote_copy(
            src_ref=outgoing.at[k],
            dst_ref=incoming.at[k],
            send_sem=edge_send.at[k],
            recv_sem=edge_recv.at[k],
            device_id=(lax.rem(node + k, nodes), group),
            device_id_type=MESH,
        )

    def send_edges(k, _):
        pick(lax.rem(node + k, nodes), outgoing.at[k])
        edge_copy(k).start()
        return 0

    lax.fori_loop(1, nodes, send_edges, 0)

    key_t = jnp.transpose(w_key[...].astype(F32)).astype(BF16)
    kv = jnp.zeros((width, width), F32)
    ksum = jnp.zeros((width, 1), F32)

    def phi(x):
        return jnp.where(x > 0.0, x + 1.0, jnp.exp(jnp.minimum(x, 0.0)))

    part = min(512, rows)

    def project(b, carry):
        kv, ksum = carry
        at = pl.ds(pl.multiple_of(b * part, part), part)
        x = feats[at, :]
        q = phi(jnp.dot(x, w_query[...], preferred_element_type=F32))
        high = q.astype(BF16)
        q_hi[at, :] = high
        q_lo[at, :] = (q - high.astype(F32)).astype(BF16)
        k = phi(lax.dot_general(key_t, x, (((1,), (1,)), ((), ())), preferred_element_type=F32))
        v = jnp.dot(x, w_value[...], preferred_element_type=F32).astype(BF16)
        kv = kv + jnp.dot(k.astype(BF16), v, preferred_element_type=F32)
        return kv, ksum + jnp.sum(k, axis=1, keepdims=True)

    kv, ksum = lax.fori_loop(0, rows // part, project, (kv, ksum))
    kv_local[:, :, 0:width] = kv.reshape(reducers, chunk, width)
    kv_local[:, :, width:] = jnp.broadcast_to(ksum, (width, 128)).reshape(reducers, chunk, 128)

    def part_copy(j):
        c = lax.rem(mine + j, reducers)
        peer = c * step
        return pltpu.make_async_remote_copy(
            src_ref=kv_local.at[c],
            dst_ref=kv_parts.at[lax.rem(me - peer - 1 + total, total)],
            send_sem=part_send.at[j],
            recv_sem=part_recv,
            device_id=(peer // groups, lax.rem(peer, groups)),
            device_id_type=MESH,
        )

    def each_part(act):
        if step > 1:
            @pl.when(jnp.logical_not(is_reducer))
            def _():
                act(part_copy(0))

        def go(j, _):
            act(part_copy(j))
            return 0

        lax.fori_loop(1, reducers, go, 0)

    each_part(lambda copy: copy.start())

    row_of = lax.broadcasted_iota(jnp.int32, (BLK, slots), 0).astype(F32).astype(BF16)

    def add_batch(first, fresh):
        weights, highs, lows = [], [], []
        for i in range(batch):
            meta = incoming[first + i, slots:slots + META, :]
            weights.append(meta[0:1, :])
            highs.append(meta[1:2, :])
            lows.append(meta[2:3, :])

        def one_block(b, _):
            at = pl.ds(pl.multiple_of(b * BLK, BLK), BLK)
            here = lax.convert_element_type(b, F32)
            sums = jnp.zeros((BLK, width), F32) if fresh else acc[at, :]
            for i in range(batch):
                local = jnp.where(highs[i].astype(F32) == here, lows[i].astype(F32), -1.0).astype(BF16)
                table = jnp.where(row_of == local, weights[i], zero)
                sums += jnp.dot(table, incoming[first + i, 0:slots, :], preferred_element_type=F32)
            acc[at, :] = sums
            return 0

        lax.fori_loop(0, blocks, one_block, 0)

    for i in range(1, batch):
        edge_copy(i).wait_recv()
    add_batch(0, True)

    def total_copy(j):
        peer = lax.rem(me + j, total)
        return pltpu.make_async_remote_copy(
            src_ref=kv_total.at[mine],
            dst_ref=kv_total.at[mine],
            send_sem=total_send,
            recv_sem=total_recv,
            device_id=(peer // groups, lax.rem(peer, groups)),
            device_id_type=MESH,
        )

    @pl.when(is_reducer)
    def _():
        pltpu.make_async_copy(kv_parts, kv_parts, part_recv).wait()
        kv_total[mine] = kv_local[mine] + jnp.sum(kv_parts[...], axis=0)

        def go(j, _):
            total_copy(j).start()
            return 0

        lax.fori_loop(1, total, go, 0)

    def rest(g, _):
        first = g * batch
        for i in range(batch):
            edge_copy(first + i).wait_recv()
        add_batch(first, False)
        return 0

    lax.fori_loop(1, nodes // batch, rest, 0)

    others = kv_total.at[pl.ds(0, reducers - 1)]
    if step > 1:
        @pl.when(is_reducer)
        def _():
            pltpu.make_async_copy(others, others, total_recv).wait()

        @pl.when(jnp.logical_not(is_reducer))
        def _():
            pltpu.make_async_copy(kv_total, kv_total, total_recv).wait()
    else:
        pltpu.make_async_copy(others, others, total_recv).wait()

    summary = kv_total[...].reshape(width, width + 128)
    s_hi = summary.astype(BF16)
    s_lo = (summary - s_hi.astype(F32)).astype(BF16)

    def finish(b, _):
        at = pl.ds(pl.multiple_of(b * BLK, BLK), BLK)
        gcn = jnp.dot(acc[at, :].astype(BF16), w_graph[...], preferred_element_type=F32)
        high, low = q_hi[at, :], q_lo[at, :]
        both = jnp.dot(high, s_hi, preferred_element_type=F32)
        both += jnp.dot(high, s_lo, preferred_element_type=F32)
        both += jnp.dot(low, s_hi, preferred_element_type=F32)
        under = 1.0 / both[:, width:]
        attn = both[:, 0:width] * jnp.concatenate([under] * (width // 128), axis=1)
        out[at, :] = (0.5 * attn + 0.5 * gcn).astype(BF16)
        return 0

    lax.fori_loop(0, blocks, finish, 0)

    def sent(k, _):
        edge_copy(k).wait_send()
        return 0

    lax.fori_loop(1, nodes, sent, 0)
    each_part(lambda copy: copy.wait_send())

    @pl.when(is_reducer)
    def _():
        pltpu.make_async_copy(kv_parts, kv_parts, total_send).wait()


def body(nodes, groups, *arrays):
    feats, src_index = arrays[0], arrays[5]
    rows, width = feats.shape
    slots = src_index.shape[3]
    total = nodes * groups
    reducers = min(total, width // 8)
    batch = 4
    edges = arrays[7].astype(F32)
    counts = arrays[8].reshape(-1)
    vmem = pl.BlockSpec(memory_space=pltpu.VMEM)
    return pl.pallas_call(
        functools.partial(kernel, nodes, groups, reducers, batch),
        out_shape=jax.ShapeDtypeStruct((rows, width), BF16),
        in_specs=[vmem] * 8 + [pl.BlockSpec(memory_space=pltpu.SMEM)],
        out_specs=vmem,
        scratch_shapes=[
            pltpu.VMEM((nodes, slots + META, width), BF16),
            pltpu.VMEM((nodes, slots + META, width), BF16),
            pltpu.VMEM((slots, nodes * 128), BF16),
            pltpu.VMEM((slots, nodes * 128), BF16),
            pltpu.VMEM((rows, width), F32),
            pltpu.VMEM((rows, width), BF16),
            pltpu.VMEM((rows, width), BF16),
            pltpu.VMEM((reducers, width // reducers, width + 128), F32),
            pltpu.VMEM((total - 1, width // reducers, width + 128), F32),
            pltpu.VMEM((reducers, width // reducers, width + 128), F32),
            pltpu.SemaphoreType.DMA((nodes,)),
            pltpu.SemaphoreType.DMA((nodes,)),
            pltpu.SemaphoreType.DMA((reducers,)),
            pltpu.SemaphoreType.DMA,
            pltpu.SemaphoreType.DMA,
            pltpu.SemaphoreType.DMA,
        ],
        compiler_params=pltpu.CompilerParams(
            collective_id=0, has_side_effects=True, vmem_limit_bytes=48 * 1024 * 1024
        ),
    )(*arrays[:7], edges, counts)


def solution(mesh):
    in_specs = (
        P(("node", "group"), None),
        P(),
        P(),
        P(),
        P(),
        P("node", "group", None, None),
        P("node", "group", None, None),
        P("node", "group", None, None),
        P("node", "group", None),
    )
    return jax.shard_map(
        functools.partial(body, mesh.shape["node"], mesh.shape["group"]),
        mesh=mesh,
        in_specs=in_specs,
        out_specs=P(("node", "group"), None),
        check_vma=False,
    )
```

```python
import functools

import jax
import jax.numpy as jnp
from jax import lax
from jax.experimental import pallas as pl
from jax.experimental.pallas import tpu as pltpu
from jax.sharding import PartitionSpec as P

TILE = 128
BLK = 256
META = 16
F32 = jnp.float32
BF16 = jnp.bfloat16
MESH = pl.DeviceIdType.MESH


def kernel(
    nodes, groups, inner, batch,
    feats_in, w_query_in, w_key_in, w_value_in, w_graph_in, src_in, dst_in, weight_in, count_in,
    out,
    feats, w_query, w_key, w_value, w_graph, src_index, dst_slot, edge_weight, tile_count, live_weight,
    outgoing, incoming, src_hi, src_lo, acc, attn, q_hi, q_lo,
    kv_local, kv_parts, kv_plane, kv_columns, kv_total,
    load_sem, edge_send, edge_recv, part_send, part_recv, column_send, column_recv, total_send, total_recv,
):
    total = nodes * groups
    plane = inner * groups
    outer = nodes // inner
    rows, width = feats.shape
    slots = src_index.shape[3]
    blocks = rows // BLK
    chunk = width // plane
    node = lax.axis_index("node")
    group = lax.axis_index("group")
    me = node * groups + group
    level = node // inner
    spot = lax.rem(node, inner) * groups + group

    loads = [
        pltpu.make_async_copy(src, dst, load_sem.at[i])
        for i, (src, dst) in enumerate((
            (src_in, src_index), (count_in, tile_count), (dst_in, dst_slot), (weight_in, edge_weight),
            (feats_in, feats), (w_query_in, w_query), (w_key_in, w_key), (w_value_in, w_value),
            (w_graph_in, w_graph),
        ))
    ]
    for load in loads:
        load.start()
    barrier = pltpu.get_barrier_semaphore()

    def greet(j, _):
        peer = lax.rem(me + j, total)
        pl.semaphore_signal(
            barrier, inc=1, device_id=(peer // groups, lax.rem(peer, groups)), device_id_type=MESH
        )
        return 0

    lax.fori_loop(1, total, greet, 0)
    for load in loads[0:4]:
        load.wait()

    sources = src_index[0, 0]
    spread = (
        lax.broadcasted_iota(jnp.int32, (nodes, nodes * 128), 0)
        == lax.broadcasted_iota(jnp.int32, (nodes, nodes * 128), 1) // 128
    ).astype(F32).astype(BF16)
    for value, ref in ((sources // BLK, src_hi), (lax.rem(sources, BLK), src_lo)):
        columns = jnp.transpose(value.astype(F32)).astype(BF16)
        ref[...] = jnp.dot(columns, spread, preferred_element_type=F32).astype(BF16)

    lanes = lax.broadcasted_iota(jnp.int32, (slots, 128), 1).astype(F32)
    lane_of = (lanes.astype(BF16), (lanes + 128.0).astype(BF16))
    one, zero = jnp.ones((), BF16), jnp.zeros((), BF16)
    tile_of = (lax.broadcasted_iota(jnp.int32, (nodes, slots), 1) // TILE).astype(F32)
    diagonal = lax.broadcasted_iota(jnp.int32, (nodes, nodes), 0) == lax.broadcasted_iota(
        jnp.int32, (nodes, nodes), 1
    )
    counts = jnp.sum(
        jnp.where(diagonal, tile_count[0].astype(F32), 0.0), axis=1, keepdims=True
    )
    live_weight[...] = jnp.where(tile_of < counts, edge_weight[0, 0].astype(F32), 0.0)
    meta_row = lax.broadcasted_iota(jnp.int32, (META, slots), 0)

    def pick(owner, put):
        start = pl.multiple_of(owner * 128, 128)
        high = src_hi[:, pl.ds(start, 128)]
        low = src_lo[:, pl.ds(start, 128)]
        picked = jnp.zeros((slots, width), F32)
        for b in range(blocks):
            local = jnp.where(high == jnp.array(b, BF16), low, jnp.array(-1.0, BF16))
            table = jnp.concatenate(
                [jnp.where(local == lane, one, zero) for lane in lane_of], axis=1
            )
            picked += jnp.dot(table, feats[b * BLK:(b + 1) * BLK, :], preferred_element_type=F32)
        put[0:slots, :] = picked.astype(BF16)
        slot = dst_slot[0, 0, pl.ds(owner, 1), :]
        weight = live_weight[pl.ds(owner, 1), :]
        meta = jnp.where(meta_row == 0, weight, 0.0)
        meta = jnp.where(meta_row == 1, (slot // BLK).astype(F32), meta)
        meta = jnp.where(meta_row == 2, lax.rem(slot, BLK).astype(F32), meta)
        put[slots:slots + META, :] = meta.astype(BF16)

    def edge_copy(k):
        return pltpu.make_async_remote_copy(
            src_ref=outgoing.at[k],
            dst_ref=incoming.at[k],
            send_sem=edge_send.at[k],
            recv_sem=edge_recv.at[k],
            device_id=(lax.rem(node + k, nodes), group),
            device_id_type=MESH,
        )

    def send_edges(k, _):
        pick(lax.rem(node + k, nodes), outgoing.at[k])
        edge_copy(k).start()
        return 0


    def phi(x):
        return jnp.where(x > 0.0, x + 1.0, jnp.exp(jnp.minimum(x, 0.0)))

    part = min(512, rows)

    def project(b, carry):
        kv, ksum = carry
        at = pl.ds(pl.multiple_of(b * part, part), part)
        x = feats[at, :]
        q = phi(jnp.dot(x, w_query[...], preferred_element_type=F32))
        high = q.astype(BF16)
        q_hi[at, :] = high
        q_lo[at, :] = (q - high.astype(F32)).astype(BF16)
        key_t = jnp.transpose(w_key[...].astype(F32)).astype(BF16)
        k = phi(lax.dot_general(key_t, x, (((1,), (1,)), ((), ())), preferred_element_type=F32))
        v = jnp.dot(x, w_value[...], preferred_element_type=F32).astype(BF16)
        kv = kv + jnp.dot(k.astype(BF16), v, preferred_element_type=F32)
        return kv, ksum + jnp.sum(k, axis=1, keepdims=True)

    def summarize():
        kv = jnp.zeros((width, width), F32)
        ksum = jnp.zeros((width, 1), F32)
        kv, ksum = lax.fori_loop(0, rows // part, project, (kv, ksum))
        kv_local[:, :, 0:width] = kv.reshape(plane, chunk, width)
        kv_local[:, :, width:] = jnp.broadcast_to(ksum, (width, 128)).reshape(plane, chunk, 128)

    def place(j):
        peer = lax.rem(spot + j, plane)
        return peer, (level * inner + peer // groups, lax.rem(peer, groups))

    def part_copy(j):
        peer, device = place(j)
        return pltpu.make_async_remote_copy(
            src_ref=kv_local.at[peer], dst_ref=kv_parts.at[j - 1],
            send_sem=part_send.at[j], recv_sem=part_recv.at[j],
            device_id=device, device_id_type=MESH,
        )

    def column_copy(j):
        return pltpu.make_async_remote_copy(
            src_ref=kv_plane, dst_ref=kv_columns.at[j - 1],
            send_sem=column_send.at[j], recv_sem=column_recv.at[j],
            device_id=(lax.rem(node + j * inner, nodes), group), device_id_type=MESH,
        )

    def total_copy(j):
        peer, device = place(j)
        return pltpu.make_async_remote_copy(
            src_ref=kv_total.at[spot], dst_ref=kv_total.at[spot],
            send_sem=total_send.at[j], recv_sem=total_recv,
            device_id=device, device_id_type=MESH,
        )

    def each(first, last, act):
        def go(j, _):
            act(j)
            return 0

        lax.fori_loop(first, last, go, 0)

    def start_parts():
        each(1, plane, lambda j: part_copy(j).start())

    def start_columns():
        each(1, plane, lambda j: part_copy(j).wait_recv())
        kv_plane[...] = kv_local[spot] + jnp.sum(kv_parts[...], axis=0)
        each(1, outer, lambda j: column_copy(j).start())

    def start_totals():
        each(1, outer, lambda j: column_copy(j).wait_recv())
        kv_total[spot] = kv_plane[...] + jnp.sum(kv_columns[...], axis=0)
        each(1, plane, lambda j: total_copy(j).start())

    def wait_totals():
        others = kv_total.at[pl.ds(0, plane - 1)]
        pltpu.make_async_copy(others, others, total_recv).wait()

    row_of = lax.broadcasted_iota(jnp.int32, (BLK, slots), 0).astype(F32).astype(BF16)

    def add_batch(first, fresh, last=False):
        weights, highs, lows = [], [], []
        for i in range(batch):
            meta = incoming[first + i, slots:slots + META, :]
            weights.append(meta[0:1, :])
            highs.append(meta[1:2, :])
            lows.append(meta[2:3, :])
        arrived = jnp.concatenate([incoming[first + i, 0:slots, :] for i in range(batch)], axis=0)

        def one_block(b, _):
            at = pl.ds(pl.multiple_of(b * BLK, BLK), BLK)
            here = lax.convert_element_type(b, F32)
            tables = []
            for i in range(batch):
                local = jnp.where(highs[i].astype(F32) == here, lows[i].astype(F32), -1.0).astype(BF16)
                tables.append(jnp.where(row_of == local, weights[i], zero))
            sums = jnp.dot(jnp.concatenate(tables, axis=1), arrived, preferred_element_type=F32)
            if last:
                agg = (acc[at, :] + sums).astype(BF16)
                gcn = jnp.dot(agg, w_graph[...], preferred_element_type=F32)
                out[at, :] = (attn[at, :] + 0.5 * gcn).astype(BF16)
            else:
                acc[at, :] = sums if fresh else acc[at, :] + sums
            return 0

        lax.fori_loop(0, blocks, one_block, 0)

    def first_batch():
        for i in range(1, batch):
            edge_copy(i).wait_recv()
        add_batch(0, True)

    def rest(g, _):
        first = g * batch
        for i in range(batch):
            edge_copy(first + i).wait_recv()
        add_batch(first, False)
        return 0

    def attend():
        summary = kv_total[...].reshape(width, width + 128)
        s_hi = summary.astype(BF16)
        s_lo = (summary - s_hi.astype(F32)).astype(BF16)

        def one_block(b, _):
            at = pl.ds(pl.multiple_of(b * BLK, BLK), BLK)
            high, low = q_hi[at, :], q_lo[at, :]
            both = jnp.dot(high, s_hi, preferred_element_type=F32)
            both += jnp.dot(high, s_lo, preferred_element_type=F32)
            both += jnp.dot(low, s_hi, preferred_element_type=F32)
            under = 0.5 / both[:, width:]
            attn[at, :] = both[:, 0:width] * jnp.concatenate([under] * (width // 128), axis=1)
            return 0

        lax.fori_loop(0, blocks, one_block, 0)

    loads[4].wait()
    pl.semaphore_wait(barrier, total - 1)
    lax.fori_loop(1, nodes, send_edges, 0)
    for load in loads[5:]:
        load.wait()
    summarize()
    start_parts()
    pick(node, incoming.at[0])
    start_columns()
    first_batch()
    start_totals()
    lax.fori_loop(1, nodes // batch - 1, rest, 0)
    wait_totals()
    attend()
    last = nodes - batch
    for i in range(batch):
        edge_copy(last + i).wait_recv()
    add_batch(last, False, True)

    def sent(k, _):
        edge_copy(k).wait_send()
        return 0

    lax.fori_loop(1, nodes, sent, 0)
    each(1, plane, lambda j: part_copy(j).wait_send())
    each(1, outer, lambda j: column_copy(j).wait_send())
    each(1, plane, lambda j: total_copy(j).wait_send())


def body(nodes, groups, *arrays):
    feats, src_index = arrays[0], arrays[5]
    rows, width = feats.shape
    slots = src_index.shape[3]
    inner = 4
    plane = inner * groups
    chunk = (width // plane, width + 128)
    hbm = pl.BlockSpec(memory_space=pltpu.HBM)
    return pl.pallas_call(
        functools.partial(kernel, nodes, groups, inner, 4),
        out_shape=jax.ShapeDtypeStruct((rows, width), BF16),
        in_specs=[hbm] * 9,
        out_specs=pl.BlockSpec(memory_space=pltpu.VMEM),
        scratch_shapes=[pltpu.VMEM(a.shape, a.dtype) for a in arrays] + [
            pltpu.VMEM((nodes, slots), F32),
            pltpu.VMEM((nodes, slots + META, width), BF16),
            pltpu.VMEM((nodes, slots + META, width), BF16),
            pltpu.VMEM((slots, nodes * 128), BF16),
            pltpu.VMEM((slots, nodes * 128), BF16),
            pltpu.VMEM((rows, width), F32),
            pltpu.VMEM((rows, width), F32),
            pltpu.VMEM((rows, width), BF16),
            pltpu.VMEM((rows, width), BF16),
            pltpu.VMEM((plane, *chunk), F32),
            pltpu.VMEM((plane - 1, *chunk), F32),
            pltpu.VMEM(chunk, F32),
            pltpu.VMEM((nodes // inner - 1, *chunk), F32),
            pltpu.VMEM((plane, *chunk), F32),
            pltpu.SemaphoreType.DMA((len(arrays),)),
            pltpu.SemaphoreType.DMA((nodes,)),
            pltpu.SemaphoreType.DMA((nodes,)),
            pltpu.SemaphoreType.DMA((plane,)),
            pltpu.SemaphoreType.DMA((plane,)),
            pltpu.SemaphoreType.DMA((nodes // inner,)),
            pltpu.SemaphoreType.DMA((nodes // inner,)),
            pltpu.SemaphoreType.DMA((plane,)),
            pltpu.SemaphoreType.DMA,
        ],
        compiler_params=pltpu.CompilerParams(
            collective_id=0, has_side_effects=True, vmem_limit_bytes=62 * 1024 * 1024
        ),
    )(*arrays)


def solution(mesh):
    in_specs = (
        P(("node", "group"), None),
        P(),
        P(),
        P(),
        P(),
        P("node", "group", None, None),
        P("node", "group", None, None),
        P("node", "group", None, None),
        P("node", "group", None),
    )
    return jax.shard_map(
        functools.partial(body, mesh.shape["node"], mesh.shape["group"]),
        mesh=mesh,
        in_specs=in_specs,
        out_specs=P(("node", "group"), None),
        check_vma=False,
    )
```

```python
import functools

import jax
import jax.numpy as jnp
from jax import lax
from jax.experimental import pallas as pl
from jax.experimental.pallas import tpu as pltpu
from jax.sharding import PartitionSpec as P

TILE = 128
BLK = 256
META = 16
F32 = jnp.float32
BF16 = jnp.bfloat16
MESH = pl.DeviceIdType.MESH


def kernel(
    nodes, groups, inner, batch,
    feats_in, w_query_in, w_key_in, w_value_in, w_graph_in, src_in, dst_in, weight_in, count_in,
    out,
    feats, w_query, w_key, w_value, w_graph, src_index, dst_slot, edge_weight, tile_count, live_weight,
    outgoing, incoming, src_hi, src_lo, acc, attn, q_hi, q_lo,
    kv_local, kv_parts, kv_plane, kv_columns, kv_total,
    load_sem, edge_send, edge_recv, part_send, part_recv, column_send, column_recv, total_send, total_recv,
):
    total = nodes * groups
    plane = inner * groups
    outer = nodes // inner
    rows, width = feats.shape
    slots = src_index.shape[3]
    blocks = rows // BLK
    chunk = width // plane
    node = lax.axis_index("node")
    group = lax.axis_index("group")
    me = node * groups + group
    level = node // inner
    spot = lax.rem(node, inner) * groups + group

    loads = [
        pltpu.make_async_copy(src, dst, load_sem.at[i])
        for i, (src, dst) in enumerate((
            (src_in, src_index), (count_in, tile_count), (dst_in, dst_slot), (weight_in, edge_weight),
            (feats_in, feats), (w_query_in, w_query), (w_key_in, w_key), (w_value_in, w_value),
            (w_graph_in, w_graph),
        ))
    ]
    for load in loads:
        load.start()
    barrier = pltpu.get_barrier_semaphore()

    def greet(j, _):
        peer = lax.rem(me + j, total)
        pl.semaphore_signal(
            barrier, inc=1, device_id=(peer // groups, lax.rem(peer, groups)), device_id_type=MESH
        )
        return 0

    lax.fori_loop(1, total, greet, 0)
    for load in loads[0:4]:
        load.wait()

    sources = src_index[0, 0]
    spread = (
        lax.broadcasted_iota(jnp.int32, (nodes, nodes * 128), 0)
        == lax.broadcasted_iota(jnp.int32, (nodes, nodes * 128), 1) // 128
    ).astype(F32).astype(BF16)
    for value, ref in ((sources // BLK, src_hi), (lax.rem(sources, BLK), src_lo)):
        columns = jnp.transpose(value.astype(F32)).astype(BF16)
        ref[...] = jnp.dot(columns, spread, preferred_element_type=F32).astype(BF16)

    lanes = lax.broadcasted_iota(jnp.int32, (slots, 128), 1).astype(F32)
    lane_of = (lanes.astype(BF16), (lanes + 128.0).astype(BF16))
    one, zero = jnp.ones((), BF16), jnp.zeros((), BF16)
    tile_of = (lax.broadcasted_iota(jnp.int32, (nodes, slots), 1) // TILE).astype(F32)
    diagonal = lax.broadcasted_iota(jnp.int32, (nodes, nodes), 0) == lax.broadcasted_iota(
        jnp.int32, (nodes, nodes), 1
    )
    counts = jnp.sum(
        jnp.where(diagonal, tile_count[0].astype(F32), 0.0), axis=1, keepdims=True
    )
    live_weight[...] = jnp.where(tile_of < counts, edge_weight[0, 0].astype(F32), 0.0)
    meta_row = lax.broadcasted_iota(jnp.int32, (META, slots), 0)

    def pick(owner, put):
        start = pl.multiple_of(owner * 128, 128)
        high = src_hi[:, pl.ds(start, 128)]
        low = src_lo[:, pl.ds(start, 128)]
        picked = jnp.zeros((slots, width), F32)
        for b in range(blocks):
            local = jnp.where(high == jnp.array(b, BF16), low, jnp.array(-1.0, BF16))
            table = jnp.concatenate(
                [jnp.where(local == lane, one, zero) for lane in lane_of], axis=1
            )
            picked += jnp.dot(table, feats[b * BLK:(b + 1) * BLK, :], preferred_element_type=F32)
        put[0:slots, :] = picked.astype(BF16)
        slot = dst_slot[0, 0, pl.ds(owner, 1), :]
        weight = live_weight[pl.ds(owner, 1), :]
        meta = jnp.where(meta_row == 0, weight, 0.0)
        meta = jnp.where(meta_row == 1, (slot // BLK).astype(F32), meta)
        meta = jnp.where(meta_row == 2, lax.rem(slot, BLK).astype(F32), meta)
        put[slots:slots + META, :] = meta.astype(BF16)

    def edge_copy(k):
        return pltpu.make_async_remote_copy(
            src_ref=outgoing.at[k],
            dst_ref=incoming.at[k],
            send_sem=edge_send.at[k],
            recv_sem=edge_recv.at[k],
            device_id=(lax.rem(node + k, nodes), group),
            device_id_type=MESH,
        )

    def send_edges(k, _):
        pick(lax.rem(node + k, nodes), outgoing.at[k])
        edge_copy(k).start()
        return 0


    def phi(x):
        return jnp.where(x > 0.0, x + 1.0, jnp.exp(jnp.minimum(x, 0.0)))

    part = min(512, rows)

    def project(b, carry):
        kv, ksum = carry
        at = pl.ds(pl.multiple_of(b * part, part), part)
        x = feats[at, :]
        q = phi(jnp.dot(x, w_query[...], preferred_element_type=F32))
        high = q.astype(BF16)
        q_hi[at, :] = high
        q_lo[at, :] = (q - high.astype(F32)).astype(BF16)
        key_t = jnp.transpose(w_key[...].astype(F32)).astype(BF16)
        k = phi(lax.dot_general(key_t, x, (((1,), (1,)), ((), ())), preferred_element_type=F32))
        v = jnp.dot(x, w_value[...], preferred_element_type=F32).astype(BF16)
        kv = kv + jnp.dot(k.astype(BF16), v, preferred_element_type=F32)
        return kv, ksum + jnp.sum(k, axis=1, keepdims=True)

    def summarize():
        kv = jnp.zeros((width, width), F32)
        ksum = jnp.zeros((width, 1), F32)
        kv, ksum = lax.fori_loop(0, rows // part, project, (kv, ksum))
        kv_local[:, :, 0:width] = kv.reshape(plane, chunk, width)
        kv_local[:, :, width:] = jnp.broadcast_to(ksum, (width, 128)).reshape(plane, chunk, 128)

    def place(j):
        peer = lax.rem(spot + j, plane)
        return peer, (level * inner + peer // groups, lax.rem(peer, groups))

    def part_copy(j):
        peer, device = place(j)
        return pltpu.make_async_remote_copy(
            src_ref=kv_local.at[peer], dst_ref=kv_parts.at[j - 1],
            send_sem=part_send.at[j], recv_sem=part_recv.at[j],
            device_id=device, device_id_type=MESH,
        )

    def column_copy(j):
        return pltpu.make_async_remote_copy(
            src_ref=kv_plane, dst_ref=kv_columns.at[j - 1],
            send_sem=column_send.at[j], recv_sem=column_recv.at[j],
            device_id=(lax.rem(node + j * inner, nodes), group), device_id_type=MESH,
        )

    def total_copy(j):
        peer, device = place(j)
        return pltpu.make_async_remote_copy(
            src_ref=kv_total.at[spot], dst_ref=kv_total.at[spot],
            send_sem=total_send.at[j], recv_sem=total_recv,
            device_id=device, device_id_type=MESH,
        )

    def each(first, last, act):
        def go(j, _):
            act(j)
            return 0

        lax.fori_loop(first, last, go, 0)

    def start_parts():
        each(1, plane, lambda j: part_copy(j).start())

    def start_columns():
        each(1, plane, lambda j: part_copy(j).wait_recv())
        kv_plane[...] = kv_local[spot] + jnp.sum(kv_parts[...], axis=0)
        each(1, outer, lambda j: column_copy(j).start())

    def start_totals():
        each(1, outer, lambda j: column_copy(j).wait_recv())
        kv_total[spot] = kv_plane[...] + jnp.sum(kv_columns[...], axis=0)
        each(1, plane, lambda j: total_copy(j).start())

    def wait_totals():
        others = kv_total.at[pl.ds(0, plane - 1)]
        pltpu.make_async_copy(others, others, total_recv).wait()

    row_of = lax.broadcasted_iota(jnp.int32, (BLK, slots), 0).astype(F32).astype(BF16)

    def add_batch(first, fresh, last=False):
        weights, highs, lows = [], [], []
        for i in range(batch):
            meta = incoming[first + i, slots:slots + META, :]
            weights.append(meta[0:1, :])
            highs.append(meta[1:2, :])
            lows.append(meta[2:3, :])
        arrived = jnp.concatenate([incoming[first + i, 0:slots, :] for i in range(batch)], axis=0)

        def one_block(b, _):
            at = pl.ds(pl.multiple_of(b * BLK, BLK), BLK)
            here = lax.convert_element_type(b, F32)
            tables = []
            for i in range(batch):
                local = jnp.where(highs[i].astype(F32) == here, lows[i].astype(F32), -1.0).astype(BF16)
                tables.append(jnp.where(row_of == local, weights[i], zero))
            sums = jnp.dot(jnp.concatenate(tables, axis=1), arrived, preferred_element_type=F32)
            if last:
                agg = (acc[at, :] + sums).astype(BF16)
                gcn = jnp.dot(agg, w_graph[...], preferred_element_type=F32)
                out[at, :] = (attn[at, :] + 0.5 * gcn).astype(BF16)
            else:
                acc[at, :] = sums if fresh else acc[at, :] + sums
            return 0

        lax.fori_loop(0, blocks, one_block, 0)

    def first_batch():
        for i in range(1, batch):
            edge_copy(i).wait_recv()
        add_batch(0, True)

    def rest(g, _):
        first = g * batch
        for i in range(batch):
            edge_copy(first + i).wait_recv()
        add_batch(first, False)
        return 0

    def attend():
        summary = kv_total[...].reshape(width, width + 128)
        s_hi = summary.astype(BF16)
        s_lo = (summary - s_hi.astype(F32)).astype(BF16)

        def one_block(b, _):
            at = pl.ds(pl.multiple_of(b * BLK, BLK), BLK)
            high, low = q_hi[at, :], q_lo[at, :]
            both = jnp.dot(high, s_hi, preferred_element_type=F32)
            both += jnp.dot(high, s_lo, preferred_element_type=F32)
            both += jnp.dot(low, s_hi, preferred_element_type=F32)
            under = 0.5 / both[:, width:]
            attn[at, :] = both[:, 0:width] * jnp.concatenate([under] * (width // 128), axis=1)
            return 0

        lax.fori_loop(0, blocks, one_block, 0)

    loads[4].wait()
    pl.semaphore_wait(barrier, total - 1)
    lax.fori_loop(1, 5, send_edges, 0)
    for load in loads[5:]:
        load.wait()
    summarize()
    start_parts()
    lax.fori_loop(5, 8, send_edges, 0)
    start_columns()
    lax.fori_loop(8, 12, send_edges, 0)
    start_totals()
    lax.fori_loop(12, nodes, send_edges, 0)
    pick(node, incoming.at[0])
    first_batch()
    lax.fori_loop(1, nodes // batch - 1, rest, 0)
    wait_totals()
    attend()
    last = nodes - batch
    for i in range(batch):
        edge_copy(last + i).wait_recv()
    add_batch(last, False, True)

    def sent(k, _):
        edge_copy(k).wait_send()
        return 0

    lax.fori_loop(1, nodes, sent, 0)
    each(1, plane, lambda j: part_copy(j).wait_send())
    each(1, outer, lambda j: column_copy(j).wait_send())
    each(1, plane, lambda j: total_copy(j).wait_send())


def body(nodes, groups, *arrays):
    feats, src_index = arrays[0], arrays[5]
    rows, width = feats.shape
    slots = src_index.shape[3]
    inner = 4
    plane = inner * groups
    chunk = (width // plane, width + 128)
    hbm = pl.BlockSpec(memory_space=pltpu.HBM)
    return pl.pallas_call(
        functools.partial(kernel, nodes, groups, inner, 4),
        out_shape=jax.ShapeDtypeStruct((rows, width), BF16),
        in_specs=[hbm] * 9,
        out_specs=pl.BlockSpec(memory_space=pltpu.VMEM),
        scratch_shapes=[pltpu.VMEM(a.shape, a.dtype) for a in arrays] + [
            pltpu.VMEM((nodes, slots), F32),
            pltpu.VMEM((nodes, slots + META, width), BF16),
            pltpu.VMEM((nodes, slots + META, width), BF16),
            pltpu.VMEM((slots, nodes * 128), BF16),
            pltpu.VMEM((slots, nodes * 128), BF16),
            pltpu.VMEM((rows, width), F32),
            pltpu.VMEM((rows, width), F32),
            pltpu.VMEM((rows, width), BF16),
            pltpu.VMEM((rows, width), BF16),
            pltpu.VMEM((plane, *chunk), F32),
            pltpu.VMEM((plane - 1, *chunk), F32),
            pltpu.VMEM(chunk, F32),
            pltpu.VMEM((nodes // inner - 1, *chunk), F32),
            pltpu.VMEM((plane, *chunk), F32),
            pltpu.SemaphoreType.DMA((len(arrays),)),
            pltpu.SemaphoreType.DMA((nodes,)),
            pltpu.SemaphoreType.DMA((nodes,)),
            pltpu.SemaphoreType.DMA((plane,)),
            pltpu.SemaphoreType.DMA((plane,)),
            pltpu.SemaphoreType.DMA((nodes // inner,)),
            pltpu.SemaphoreType.DMA((nodes // inner,)),
            pltpu.SemaphoreType.DMA((plane,)),
            pltpu.SemaphoreType.DMA,
        ],
        compiler_params=pltpu.CompilerParams(
            collective_id=0, has_side_effects=True, vmem_limit_bytes=62 * 1024 * 1024
        ),
    )(*arrays)


def solution(mesh):
    in_specs = (
        P(("node", "group"), None),
        P(),
        P(),
        P(),
        P(),
        P("node", "group", None, None),
        P("node", "group", None, None),
        P("node", "group", None, None),
        P("node", "group", None),
    )
    return jax.shard_map(
        functools.partial(body, mesh.shape["node"], mesh.shape["group"]),
        mesh=mesh,
        in_specs=in_specs,
        out_specs=P(("node", "group"), None),
        check_vma=False,
    )
```

```python
import functools

import jax
import jax.numpy as jnp
from jax import lax
from jax.experimental import pallas as pl
from jax.experimental.pallas import tpu as pltpu
from jax.sharding import PartitionSpec as P

TILE = 128
BLK = 256
META = 16
F32 = jnp.float32
BF16 = jnp.bfloat16
MESH = pl.DeviceIdType.MESH


def kernel(
    nodes, groups, inner, batch,
    feats_in, w_query_in, w_key_in, w_value_in, w_graph_in, src_in, dst_in, weight_in, count_in,
    out,
    feats, w_query, w_key, w_value, w_graph, src_index, dst_slot, edge_weight, tile_count, live_weight,
    outgoing, incoming, src_hi, src_lo, acc, attn, q_hi, q_lo,
    kv_local, kv_parts, kv_plane, kv_columns, kv_total,
    load_sem, edge_send, edge_recv, part_send, part_recv, column_send, column_recv, total_send, total_recv,
    back_send, back_recv,
):
    total = nodes * groups
    plane = inner * groups
    outer = nodes // inner
    rows, width = feats.shape
    slots = src_index.shape[3]
    blocks = rows // BLK
    chunk = width // plane
    sub = chunk // outer
    halved = sub % 8 == 0
    node = lax.axis_index("node")
    group = lax.axis_index("group")
    me = node * groups + group
    level = node // inner
    spot = lax.rem(node, inner) * groups + group

    loads = [
        pltpu.make_async_copy(src, dst, load_sem.at[i])
        for i, (src, dst) in enumerate((
            (src_in, src_index), (count_in, tile_count), (dst_in, dst_slot), (weight_in, edge_weight),
            (feats_in, feats), (w_query_in, w_query), (w_key_in, w_key), (w_value_in, w_value),
            (w_graph_in, w_graph),
        ))
    ]
    for load in loads:
        load.start()
    barrier = pltpu.get_barrier_semaphore()

    def greet(j, _):
        peer = lax.rem(me + j, total)
        pl.semaphore_signal(
            barrier, inc=1, device_id=(peer // groups, lax.rem(peer, groups)), device_id_type=MESH
        )
        return 0

    lax.fori_loop(1, total, greet, 0)
    for load in loads[0:4]:
        load.wait()

    sources = src_index[0, 0]
    spread = (
        lax.broadcasted_iota(jnp.int32, (nodes, nodes * 128), 0)
        == lax.broadcasted_iota(jnp.int32, (nodes, nodes * 128), 1) // 128
    ).astype(F32).astype(BF16)
    for value, ref in ((sources // BLK, src_hi), (lax.rem(sources, BLK), src_lo)):
        columns = jnp.transpose(value.astype(F32)).astype(BF16)
        ref[...] = jnp.dot(columns, spread, preferred_element_type=F32).astype(BF16)

    lanes = lax.broadcasted_iota(jnp.int32, (slots, 128), 1).astype(F32)
    lane_of = (lanes.astype(BF16), (lanes + 128.0).astype(BF16))
    one, zero = jnp.ones((), BF16), jnp.zeros((), BF16)
    tile_of = (lax.broadcasted_iota(jnp.int32, (nodes, slots), 1) // TILE).astype(F32)
    diagonal = lax.broadcasted_iota(jnp.int32, (nodes, nodes), 0) == lax.broadcasted_iota(
        jnp.int32, (nodes, nodes), 1
    )
    counts = jnp.sum(
        jnp.where(diagonal, tile_count[0].astype(F32), 0.0), axis=1, keepdims=True
    )
    live_weight[...] = jnp.where(tile_of < counts, edge_weight[0, 0].astype(F32), 0.0)
    meta_row = lax.broadcasted_iota(jnp.int32, (META, slots), 0)

    def pick(owner, put):
        start = pl.multiple_of(owner * 128, 128)
        high = src_hi[:, pl.ds(start, 128)]
        low = src_lo[:, pl.ds(start, 128)]
        picked = jnp.zeros((slots, width), F32)
        for b in range(blocks):
            local = jnp.where(high == jnp.array(b, BF16), low, jnp.array(-1.0, BF16))
            table = jnp.concatenate(
                [jnp.where(local == lane, one, zero) for lane in lane_of], axis=1
            )
            picked += jnp.dot(table, feats[b * BLK:(b + 1) * BLK, :], preferred_element_type=F32)
        put[0:slots, :] = picked.astype(BF16)
        slot = dst_slot[0, 0, pl.ds(owner, 1), :]
        weight = live_weight[pl.ds(owner, 1), :]
        meta = jnp.where(meta_row == 0, weight, 0.0)
        meta = jnp.where(meta_row == 1, (slot // BLK).astype(F32), meta)
        meta = jnp.where(meta_row == 2, lax.rem(slot, BLK).astype(F32), meta)
        put[slots:slots + META, :] = meta.astype(BF16)

    def edge_copy(k):
        return pltpu.make_async_remote_copy(
            src_ref=outgoing.at[k],
            dst_ref=incoming.at[k],
            send_sem=edge_send.at[k],
            recv_sem=edge_recv.at[k],
            device_id=(lax.rem(node + k, nodes), group),
            device_id_type=MESH,
        )

    def send_edges(k, _):
        pick(lax.rem(node + k, nodes), outgoing.at[k])
        edge_copy(k).start()
        return 0


    def phi(x):
        return jnp.where(x > 0.0, x + 1.0, jnp.exp(jnp.minimum(x, 0.0)))

    part = min(512, rows)

    def project(b, carry):
        kv, ksum = carry
        at = pl.ds(pl.multiple_of(b * part, part), part)
        x = feats[at, :]
        q = phi(jnp.dot(x, w_query[...], preferred_element_type=F32))
        high = q.astype(BF16)
        q_hi[at, :] = high
        q_lo[at, :] = (q - high.astype(F32)).astype(BF16)
        key_t = jnp.transpose(w_key[...].astype(F32)).astype(BF16)
        k = phi(lax.dot_general(key_t, x, (((1,), (1,)), ((), ())), preferred_element_type=F32))
        v = jnp.dot(x, w_value[...], preferred_element_type=F32).astype(BF16)
        kv = kv + jnp.dot(k.astype(BF16), v, preferred_element_type=F32)
        return kv, ksum + jnp.sum(k, axis=1, keepdims=True)

    def summarize():
        kv = jnp.zeros((width, width), F32)
        ksum = jnp.zeros((width, 1), F32)
        kv, ksum = lax.fori_loop(0, rows // part, project, (kv, ksum))
        kv_local[:, :, 0:width] = kv.reshape(plane, chunk, width)
        kv_local[:, :, width:] = jnp.broadcast_to(ksum, (width, 128)).reshape(plane, chunk, 128)

    def place(j):
        peer = lax.rem(spot + j, plane)
        return peer, (level * inner + peer // groups, lax.rem(peer, groups))

    def part_copy(j):
        peer, device = place(j)
        return pltpu.make_async_remote_copy(
            src_ref=kv_local.at[peer], dst_ref=kv_parts.at[j - 1],
            send_sem=part_send.at[j], recv_sem=part_recv.at[j],
            device_id=device, device_id_type=MESH,
        )

    def column_copy(j):
        return pltpu.make_async_remote_copy(
            src_ref=kv_plane.at[pl.ds(lax.rem(level + j, outer) * sub, sub)] if halved else kv_plane,
            dst_ref=kv_columns.at[j - 1, pl.ds(0, sub)] if halved else kv_columns.at[j - 1],
            send_sem=column_send.at[j], recv_sem=column_recv.at[j],
            device_id=(lax.rem(node + j * inner, nodes), group), device_id_type=MESH,
        )

    def back_copy(j):
        own = kv_total.at[spot, pl.ds(level * sub, sub)]
        return pltpu.make_async_remote_copy(
            src_ref=own, dst_ref=own, send_sem=back_send.at[j], recv_sem=back_recv.at[j],
            device_id=(lax.rem(node + j * inner, nodes), group), device_id_type=MESH,
        )

    def start_back():
        if halved:
            each(1, outer, lambda j: column_copy(j).wait_recv())
            at = pl.ds(pl.multiple_of(level * sub, 8), sub)
            kv_total[spot, at, :] = kv_plane[at, :] + jnp.sum(kv_columns[:, 0:sub, :], axis=0)
            each(1, outer, lambda j: back_copy(j).start())

    def total_copy(j):
        peer, device = place(j)
        return pltpu.make_async_remote_copy(
            src_ref=kv_total.at[spot], dst_ref=kv_total.at[spot],
            send_sem=total_send.at[j], recv_sem=total_recv,
            device_id=device, device_id_type=MESH,
        )

    def each(first, last, act):
        def go(j, _):
            act(j)
            return 0

        lax.fori_loop(first, last, go, 0)

    def start_parts():
        each(1, plane, lambda j: part_copy(j).start())

    def start_columns():
        each(1, plane, lambda j: part_copy(j).wait_recv())
        kv_plane[...] = kv_local[spot] + jnp.sum(kv_parts[...], axis=0)
        each(1, outer, lambda j: column_copy(j).start())

    def start_totals():
        if halved:
            each(1, outer, lambda j: back_copy(j).wait_recv())
        else:
            each(1, outer, lambda j: column_copy(j).wait_recv())
            kv_total[spot] = kv_plane[...] + jnp.sum(kv_columns[...], axis=0)
        each(1, plane, lambda j: total_copy(j).start())

    def wait_totals():
        others = kv_total.at[pl.ds(0, plane - 1)]
        pltpu.make_async_copy(others, others, total_recv).wait()

    row_of = lax.broadcasted_iota(jnp.int32, (BLK, slots), 0).astype(F32).astype(BF16)

    def add_batch(first, fresh, last=False):
        weights, highs, lows = [], [], []
        for i in range(batch):
            meta = incoming[first + i, slots:slots + META, :]
            weights.append(meta[0:1, :])
            highs.append(meta[1:2, :])
            lows.append(meta[2:3, :])
        arrived = jnp.concatenate([incoming[first + i, 0:slots, :] for i in range(batch)], axis=0)

        def one_block(b, _):
            at = pl.ds(pl.multiple_of(b * BLK, BLK), BLK)
            here = lax.convert_element_type(b, F32)
            tables = []
            for i in range(batch):
                local = jnp.where(highs[i].astype(F32) == here, lows[i].astype(F32), -1.0).astype(BF16)
                tables.append(jnp.where(row_of == local, weights[i], zero))
            sums = jnp.dot(jnp.concatenate(tables, axis=1), arrived, preferred_element_type=F32)
            if last:
                agg = (acc[at, :] + sums).astype(BF16)
                gcn = jnp.dot(agg, w_graph[...], preferred_element_type=F32)
                out[at, :] = (attn[at, :] + 0.5 * gcn).astype(BF16)
            else:
                acc[at, :] = sums if fresh else acc[at, :] + sums
            return 0

        lax.fori_loop(0, blocks, one_block, 0)

    def first_batch():
        for i in range(1, batch):
            edge_copy(i).wait_recv()
        add_batch(0, True)

    def rest(g, _):
        first = g * batch
        for i in range(batch):
            edge_copy(first + i).wait_recv()
        add_batch(first, False)
        return 0

    def attend():
        summary = kv_total[...].reshape(width, width + 128)
        s_hi = summary.astype(BF16)
        s_lo = (summary - s_hi.astype(F32)).astype(BF16)

        def one_block(b, _):
            at = pl.ds(pl.multiple_of(b * BLK, BLK), BLK)
            high, low = q_hi[at, :], q_lo[at, :]
            both = jnp.dot(high, s_hi, preferred_element_type=F32)
            both += jnp.dot(high, s_lo, preferred_element_type=F32)
            both += jnp.dot(low, s_hi, preferred_element_type=F32)
            under = 0.5 / both[:, width:]
            attn[at, :] = both[:, 0:width] * jnp.concatenate([under] * (width // 128), axis=1)
            return 0

        lax.fori_loop(0, blocks, one_block, 0)

    loads[4].wait()
    pl.semaphore_wait(barrier, total - 1)
    lax.fori_loop(1, 5, send_edges, 0)
    for load in loads[5:]:
        load.wait()
    summarize()
    start_parts()
    lax.fori_loop(5, 8, send_edges, 0)
    start_columns()
    lax.fori_loop(8, 11, send_edges, 0)
    start_back()
    lax.fori_loop(11, 14, send_edges, 0)
    start_totals()
    lax.fori_loop(14, nodes, send_edges, 0)
    pick(node, incoming.at[0])
    first_batch()
    lax.fori_loop(1, nodes // batch - 1, rest, 0)
    wait_totals()
    attend()
    last = nodes - batch
    for i in range(batch):
        edge_copy(last + i).wait_recv()
    add_batch(last, False, True)

    def sent(k, _):
        edge_copy(k).wait_send()
        return 0

    lax.fori_loop(1, nodes, sent, 0)
    each(1, plane, lambda j: part_copy(j).wait_send())
    each(1, outer, lambda j: column_copy(j).wait_send())
    each(1, plane, lambda j: total_copy(j).wait_send())
    if halved:
        each(1, outer, lambda j: back_copy(j).wait_send())


def body(nodes, groups, *arrays):
    feats, src_index = arrays[0], arrays[5]
    rows, width = feats.shape
    slots = src_index.shape[3]
    inner = 4
    plane = inner * groups
    chunk = (width // plane, width + 128)
    hbm = pl.BlockSpec(memory_space=pltpu.HBM)
    return pl.pallas_call(
        functools.partial(kernel, nodes, groups, inner, 4),
        out_shape=jax.ShapeDtypeStruct((rows, width), BF16),
        in_specs=[hbm] * 9,
        out_specs=pl.BlockSpec(memory_space=pltpu.VMEM),
        scratch_shapes=[pltpu.VMEM(a.shape, a.dtype) for a in arrays] + [
            pltpu.VMEM((nodes, slots), F32),
            pltpu.VMEM((nodes, slots + META, width), BF16),
            pltpu.VMEM((nodes, slots + META, width), BF16),
            pltpu.VMEM((slots, nodes * 128), BF16),
            pltpu.VMEM((slots, nodes * 128), BF16),
            pltpu.VMEM((rows, width), F32),
            pltpu.VMEM((rows, width), F32),
            pltpu.VMEM((rows, width), BF16),
            pltpu.VMEM((rows, width), BF16),
            pltpu.VMEM((plane, *chunk), F32),
            pltpu.VMEM((plane - 1, *chunk), F32),
            pltpu.VMEM(chunk, F32),
            pltpu.VMEM((nodes // inner - 1, *chunk), F32),
            pltpu.VMEM((plane, *chunk), F32),
            pltpu.SemaphoreType.DMA((len(arrays),)),
            pltpu.SemaphoreType.DMA((nodes,)),
            pltpu.SemaphoreType.DMA((nodes,)),
            pltpu.SemaphoreType.DMA((plane,)),
            pltpu.SemaphoreType.DMA((plane,)),
            pltpu.SemaphoreType.DMA((nodes // inner,)),
            pltpu.SemaphoreType.DMA((nodes // inner,)),
            pltpu.SemaphoreType.DMA((plane,)),
            pltpu.SemaphoreType.DMA,
            pltpu.SemaphoreType.DMA((nodes // inner,)),
            pltpu.SemaphoreType.DMA((nodes // inner,)),
        ],
        compiler_params=pltpu.CompilerParams(
            collective_id=0, has_side_effects=True, vmem_limit_bytes=62 * 1024 * 1024
        ),
    )(*arrays)


def solution(mesh):
    in_specs = (
        P(("node", "group"), None),
        P(),
        P(),
        P(),
        P(),
        P("node", "group", None, None),
        P("node", "group", None, None),
        P("node", "group", None, None),
        P("node", "group", None),
    )
    return jax.shard_map(
        functools.partial(body, mesh.shape["node"], mesh.shape["group"]),
        mesh=mesh,
        in_specs=in_specs,
        out_specs=P(("node", "group"), None),
        check_vma=False,
    )
```
